256 devices in a mesh: tm: 32 (over x, z_lo, core), tok: 8 (over y, z_hi).
Axes of the slice: x: 4, y: 4, z: 8 (z_hi: 2, z_lo: 4; z = z_hi * 4 + z_lo), core: 2. Of those that a mesh axis runs over, the one named last changes fastest.
Arguments:
- tokens: bfloat16 [32, 832, 512], P('tm', 'tok'), may hold values from -41 to 41
- attn_gain: float32 [512], replicated, may hold values from 0.1 to 1.9
- query_weight: bfloat16 [512, 512], replicated, may hold values from -2 to 2
- key_weight: bfloat16 [512, 512], replicated, may hold values from -2 to 2
- value_weight: bfloat16 [512, 512], replicated, may hold values from -0.25 to 0.25
- out_weight: bfloat16 [512, 512], replicated, may hold values from -0.25 to 0.25
- first_gain: float32 [512], replicated, may hold values from 0.1 to 1.9
- first_conv: bfloat16 [3, 3, 3, 512, 512], P(None, None, None, None, 'tok'), may hold values from -0.0546875 to 0.0546875
- second_gain: float32 [512], P('tok'), may hold values from 0.1 to 1.9
- second_conv: bfloat16 [3, 3, 3, 512, 512], P(None, None, None, 'tok'), may hold values from -0.0546875 to 0.0546875
Outputs:
- mixed: bfloat16 [32, 832, 512], P('tm', 'tok')
The draws below stay inside these ranges and needn't reach their ends.
All inputs are finite; a program needn't handle non-finite values.
Results may differ from the reference program's by a relative error of at most 0.012.
Values may be sent and summed in bfloat16 or wider, within the bound.
A program may use at most 64 MiB of HBM per device.

```python
import math
import jax
import jax.numpy as jnp
from jax import lax

C = 512
GROUPS = 32
ROWS = 8
COLS = 104
FRAMES = 32


def draw_tokens(key, part):
    key = jax.random.fold_in(key, 5)
    subkeys = jax.random.split(key, 3)
    full_shape = (FRAMES, ROWS * COLS, C)
    position = jnp.arange(ROWS * COLS, dtype=jnp.float32) / (ROWS * COLS)
    jitter = jax.random.uniform(subkeys[1], (FRAMES, ROWS * COLS), jnp.float32)
    row_scale = 10.0 ** (0.5 * position[None, :] + 0.5 * jitter - 0.5)
    chan_scale = 10.0 ** (jax.random.uniform(subkeys[2], (C,), jnp.float32) - 0.5)
    basic_field = jnp.clip(jax.random.normal(subkeys[0], full_shape, jnp.float32), -4.0, 4.0)
    values_out = basic_field * row_scale[:, :, None] * chan_scale
    return jnp.clip(values_out, -41.0, 41.0).astype(jnp.bfloat16)


def draw_query_weight(key, part):
    key = jax.random.fold_in(key, 17)
    values_out = jnp.clip(jax.random.normal(key, (C, C), jnp.float32), -4.0, 4.0)
    return (values_out / math.sqrt(C)).astype(jnp.bfloat16)


def draw_key_weight(key, part):
    key = jax.random.fold_in(key, 29)
    noise_part = jnp.clip(jax.random.normal(key, (C, C), jnp.float32), -4.0, 4.0)
    values_out = noise_part
    return (values_out / math.sqrt(C)).astype(jnp.bfloat16)


def levels(stream_key, extent, pieces, low, largest):
    def one(dim, parts):
        steps = jax.random.uniform(jax.random.fold_in(jax.random.fold_in(stream_key, 6), dim), (parts,), jnp.float32, low / len(pieces), largest / len(pieces))
        return jnp.repeat(jnp.exp(steps), extent[dim] // parts).reshape((-1,) + (1,) * (len(extent) - dim - 1))

    loudness = one(*pieces[0])
    for cut in pieces[1:]:
        loudness = loudness * one(*cut)
    return loudness


def gaussian(rng, shape, spread, most, shards=(), held_as=jnp.bfloat16):
    values = spread * jax.random.normal(rng, shape, jnp.float32)
    if shards:
        values = values * levels(rng, shape, shards, -0.22, 0.18)
    return jnp.clip(values, -most, most).astype(held_as)


def setup_inputs(seed: int = 0) -> dict:
    arg_keys = jax.random.split(jax.random.key(seed), 11)
    tokens = draw_tokens(jax.random.fold_in(arg_keys[10], 71), 0)
    attn_gain = jnp.clip(1.0 + 0.18 * jax.random.normal(arg_keys[1], (C,), jnp.float32), 0.1, 1.9)
    query_weight = draw_query_weight(jax.random.fold_in(arg_keys[10], 71), 0)
    key_weight = draw_key_weight(jax.random.fold_in(arg_keys[10], 71), 0)
    value_weight = gaussian(arg_keys[4], (C, C), C ** -0.5, 0.25)
    out_weight = gaussian(arg_keys[5], (C, C), C ** -0.5, 0.25)
    first_gain = jnp.clip(1.0 + 0.18 * jax.random.normal(arg_keys[6], (C,), jnp.float32), 0.1, 1.9)
    first_conv = gaussian(arg_keys[7], (3, 3, 3, C, C), (27 * C) ** -0.5, 0.0546875, ((4, 8),))
    second_gain = jnp.clip(1.0 + 0.18 * jax.random.normal(arg_keys[8], (C,), jnp.float32), 0.1, 1.9)
    second_conv = gaussian(arg_keys[9], (3, 3, 3, C, C), (27 * C) ** -0.5, 0.0546875, ((3, 8),))
    return {"tokens": tokens, "attn_gain": attn_gain, "query_weight": query_weight, "key_weight": key_weight, "value_weight": value_weight, "out_weight": out_weight, "first_gain": first_gain, "first_conv": first_conv, "second_gain": second_gain, "second_conv": second_conv}


EPSILON = 1e-06

def local_sums(values_in, group_width):
    dims_in = values_in.shape
    grouped = values_in.reshape(dims_in[:-1] + (dims_in[-1] // group_width, group_width))
    return (lax.optimization_barrier(jnp.sum(grouped, axis=(-3, -1))), lax.optimization_barrier(jnp.sum(grouped * grouped, axis=(-3, -1))))

def group_moments(totals, squares, entries):
    group_mean = totals / entries
    return (group_mean, squares / entries - group_mean * group_mean)

def normalize(values_in, group_mean, group_var, gain, group_width):
    dims_in = values_in.shape
    grouped = values_in.reshape(dims_in[:-1] + (dims_in[-1] // group_width, group_width))
    scaled = (grouped - group_mean[..., None, :, None]) * lax.rsqrt(group_var + EPSILON)[..., None, :, None]
    return scaled.reshape(dims_in) * gain

def causal_conv(activation, kernel):
    in_ch = activation.shape[2]
    out_ch = kernel.shape[4]
    grid = activation.reshape(FRAMES, ROWS, COLS, in_ch)
    padded = jnp.pad(grid, ((2, 0), (1, 1), (1, 1), (0, 0)), mode='edge')

    def one_frame(frame_at):
        result = jnp.zeros((ROWS * COLS, out_ch), jnp.float32)
        for time_tap in range(3):
            plane = lax.dynamic_index_in_dim(padded, frame_at + time_tap, 0, keepdims=False)
            for row_tap in range(3):
                for col_tap in range(3):
                    window = plane[row_tap:row_tap + ROWS, col_tap:col_tap + COLS].reshape(ROWS * COLS, in_ch)
                    result = result + jnp.dot(window, kernel[time_tap, row_tap, col_tap], preferred_element_type=jnp.float32)
        return result
    return lax.map(one_frame, jnp.arange(FRAMES, dtype=jnp.int32))

def reference(tokens, attn_gain, query_weight, key_weight, value_weight, out_weight, first_gain, first_conv, second_gain, second_conv):
    group_width = C // GROUPS
    score_scale = 1.0 / math.sqrt(C)

    def attend_frame(frame):
        values_in = frame.astype(jnp.float32)
        totals, squares = local_sums(values_in, group_width)
        group_mean, group_var = group_moments(totals, squares, values_in.shape[0] * group_width)
        normed = normalize(values_in, group_mean, group_var, attn_gain, group_width).astype(jnp.bfloat16)
        queries = jnp.dot(normed, query_weight, preferred_element_type=jnp.float32).astype(jnp.bfloat16)
        key_rows = jnp.dot(normed, key_weight, preferred_element_type=jnp.float32).astype(jnp.bfloat16)
        value_rows = jnp.dot(normed, value_weight, preferred_element_type=jnp.float32).astype(jnp.bfloat16)
        scores = lax.dot_general(queries, key_rows, (((1,), (1,)), ((), ())), preferred_element_type=jnp.float32) * score_scale
        row_max = lax.optimization_barrier(jnp.max(scores, axis=1))
        exponent = jnp.exp(scores - row_max[:, None])
        running_sum = lax.optimization_barrier(jnp.sum(exponent, axis=1))
        weighted = jnp.dot(exponent.astype(jnp.bfloat16), value_rows, preferred_element_type=jnp.float32)
        context = (weighted / running_sum[:, None]).astype(jnp.bfloat16)
        return (values_in + jnp.dot(context, out_weight, preferred_element_type=jnp.float32)).astype(jnp.bfloat16)
    attended = lax.map(attend_frame, tokens)

    def activate(frame, gain):
        values_in = frame.astype(jnp.float32)
        totals, squares = local_sums(values_in, group_width)
        group_mean, group_var = group_moments(totals, squares, values_in.shape[0] * group_width)
        return jax.nn.silu(normalize(values_in, group_mean, group_var, gain, group_width)).astype(jnp.bfloat16)
    first_act = lax.map(lambda frame: activate(frame, first_gain), attended)
    hidden = causal_conv(first_act, first_conv)
    second_act = lax.map(lambda frame: activate(frame, second_gain), hidden)
    conv_out = causal_conv(second_act, second_conv)
    return (attended.astype(jnp.float32) + conv_out).astype(jnp.bfloat16)
```

```python
import math

import jax
import jax.numpy as jnp
from jax import lax
from jax.experimental import pallas as pl
from jax.experimental.pallas import tpu as pltpu
from jax.sharding import PartitionSpec as P

F32 = jnp.float32
BF16 = jnp.bfloat16
MESH = pl.DeviceIdType.MESH

C = 512
HALF = C // 2
ROWS = 8
COLS = 104
CELLS = ROWS * COLS
WIDTH = 16
LOCAL = 64
EPSILON = 1e-06

PAIRS = ((0, 0), (0, 2), (1, 0), (1, 2), (2, 0), (2, 2), (0, 1), (1, 1))
LAST = (2, 1)


def taps_of(time):
    return tuple((time,) + pair for pair in PAIRS)


FIRST_ORDER = (
    taps_of(0) + ((0,) + LAST, (1,) + LAST) + taps_of(1) + taps_of(2) + ((2,) + LAST,)
)
SECOND_ORDER = (
    taps_of(2) + taps_of(1) + taps_of(0) + ((1,) + LAST, (0,) + LAST, (2,) + LAST)
)
FIRST_PLACES = ((0, 512, 0), (640, 512, 1), (1152, 1664, 0))


def lane_low(shape):
    return lax.broadcasted_iota(jnp.int32, shape, len(shape) - 1) < 64


def row_before(x):
    return jnp.concatenate([x[0:1], x[0 : ROWS - 1]], axis=0)


def row_after(x):
    return jnp.concatenate([x[1:ROWS], x[ROWS - 1 : ROWS]], axis=0)


def col_before_after(x):
    col = lax.broadcasted_iota(jnp.int32, x.shape, 1)
    before = jnp.where(col == 0, x, pltpu.roll(x, 1, 1))
    after = jnp.where(col == COLS - 1, x, pltpu.roll(x, COLS - 1, 1))
    return jnp.where(lane_low(x.shape), before, after)


def group_matrix(period):
    i = lax.broadcasted_iota(jnp.int32, (128, 128), 0)
    k = lax.broadcasted_iota(jnp.int32, (128, 128), 1)
    same = ((i & (period - 1)) >> 4) == ((k & (period - 1)) >> 4)
    return jnp.where(same, 1.0, 0.0).astype(F32)


def moments(stacked, period, entries, n):
    totals = (
        jnp.dot(
            stacked,
            group_matrix(period),
            precision=lax.Precision.HIGHEST,
            preferred_element_type=F32,
        )
        / entries
    )
    mean = totals[0:n]
    var = totals[n : 2 * n] - mean * mean
    return mean, lax.rsqrt(var + EPSILON)


def wide_moments(total, square):
    pieces = [total[:, 128 * k : 128 * k + 128] for k in range(4)]
    pieces += [square[:, 128 * k : 128 * k + 128] for k in range(4)]
    mean, rstd = moments(jnp.concatenate(pieces, axis=0), 128, CELLS * WIDTH, 4)
    spread = lambda v: jnp.concatenate([v[k : k + 1] for k in range(4)], axis=1)
    return spread(mean), spread(rstd)


def silu(v):
    return v * (0.5 * jnp.tanh(0.5 * v) + 0.5)


def dot(a, b):
    return jnp.dot(a, b, preferred_element_type=F32)


def dot_t(a, b):
    return lax.dot_general(a, b, (((1,), (1,)), ((), ())), preferred_element_type=F32)


def kernel(
    tok, gain0, wq, wk, wv, wo, gain1, k1, gain2, k2, out,
    xg, x32, nb, wts, wm, wn, w1r, w1t, w2, gains, gain2v, act, zs, msg, acc, xown, xrest,
    ua, in1, in2, rs1s, rs1r, rs2s, rs2r, zsend, zrecv,
    load_sem, ag_send, ag_recv, fx_send, fx_recv, rs_send, rs_recv,
):
    me = lax.axis_index("tok")
    t = lax.axis_index("tm")
    frames = lax.axis_size("tm")
    y = me // 2
    h = me % 2
    o = 1 - h
    yp, ym, y2 = (y + 1) % 4, (y + 3) % 4, (y + 2) % 4
    up, down, across = 2 * yp + h, 2 * ym + h, 2 * y + o

    own = [
        pltpu.make_async_copy(
            tok.at[0, :, pl.ds(HALF * k, HALF)], xg.at[me, k], load_sem.at[k]
        )
        for k in range(2)
    ]
    for c in own:
        c.start()

    barrier = pltpu.get_barrier_semaphore()
    for there in (up, down, across):
        pl.semaphore_signal(barrier, inc=1, device_id={"tok": there}, device_id_type=MESH)

    @pl.when(t >= 1)
    def _():
        pl.semaphore_signal(barrier, inc=1, device_id={"tm": t - 1}, device_id_type=MESH)

    @pl.when(t >= 2)
    def _():
        pl.semaphore_signal(barrier, inc=1, device_id={"tm": t - 2}, device_id_type=MESH)

    small = [
        pltpu.make_async_copy(gain0, gains.at[0], load_sem.at[2]),
        pltpu.make_async_copy(gain1, gains.at[1], load_sem.at[3]),
        pltpu.make_async_copy(gain2, gain2v, load_sem.at[4]),
    ]
    mats = [
        pltpu.make_async_copy(w, wts.at[k], load_sem.at[5 + k])
        for k, w in enumerate((wq, wk, wv, wo))
    ]
    for c in mats + small:
        c.start()
    for k, (a, b, e) in enumerate(FIRST_ORDER):
        pltpu.make_async_copy(
            k1.at[a, b, e], w1r.at[pl.ds(LOCAL * k, LOCAL)], load_sem.at[9]
        ).start()
    for k, (a, b, e) in enumerate(SECOND_ORDER):
        pltpu.make_async_copy(
            k2.at[a, b, e], w2.at[pl.ds(LOCAL * k, LOCAL)], load_sem.at[10]
        ).start()

    def ag(block, half, there, k):
        return pltpu.make_async_remote_copy(
            src_ref=xg.at[block, half],
            dst_ref=xg.at[block, half],
            send_sem=ag_send.at[k],
            recv_sem=ag_recv.at[block, half],
            device_id={"tok": there},
            device_id_type=MESH,
        )

    gathered = []

    def ag_go(block, half, there):
        c = ag(block, half, there, len(gathered))
        c.start()
        gathered.append(c)

    def ag_wait(block, half):
        ag(block, half, across, 0).wait_recv()

    for c in own:
        c.wait()
    late = jnp.where(t < frames - 1, 1, 0) + jnp.where(t < frames - 2, 1, 0)
    pl.semaphore_wait(barrier, 3 + late)

    ag_go(me, 0, up)
    ag_go(me, 1, down)
    ag_go(me, 0, across)
    ag_go(me, 1, across)
    ag_go(me, 1, up)
    ag_go(me, 0, down)

    for c in mats[:2]:
        c.wait()
    wm[...] = (dot_t(wts[0], wts[1]) * (math.log2(math.e) / math.sqrt(C))).astype(BF16)

    ag_wait(2 * ym + h, 0)
    ag_go(2 * ym + h, 0, up)
    ag_wait(2 * yp + h, 1)
    ag_go(2 * yp + h, 1, down)

    for c in mats[2:]:
        c.wait()
    wn[...] = dot(wts[2], wts[3]).astype(BF16)

    ag_wait(across, 0)
    ag_go(across, 0, up)
    ag_go(across, 0, down)
    ag_wait(across, 1)
    ag_go(across, 1, down)
    ag_go(across, 1, up)

    pltpu.make_async_copy(w1r, w1r, load_sem.at[9]).wait()
    w1t[...] = w1r[...].T

    ag_wait(2 * ym + o, 0)
    ag_go(2 * ym + o, 0, up)
    ag_wait(2 * yp + o, 1)
    ag_go(2 * yp + o, 1, down)

    ag_wait(2 * ym + h, 1)
    ag_wait(2 * yp + h, 0)
    ag_wait(2 * y2 + h, 0)
    ag_wait(2 * y2 + h, 1)
    ag_wait(2 * ym + o, 1)
    ag_wait(2 * yp + o, 0)
    ag_wait(2 * y2 + o, 0)
    ag_wait(2 * y2 + o, 1)

    for c in small:
        c.wait()

    def collect(j, carry):
        total, square = carry
        rows = pl.ds(pl.multiple_of(j * COLS, 8), COLS)
        v = jnp.concatenate([xg[j, 0].astype(F32), xg[j, 1].astype(F32)], axis=1)
        x32[rows, :] = v
        return (
            total + jnp.sum(v, axis=0, keepdims=True),
            square + jnp.sum(v * v, axis=0, keepdims=True),
        )

    zero = jnp.zeros((1, C), F32)
    mean, rstd = wide_moments(*lax.fori_loop(0, ROWS, collect, (zero, zero)))
    scale = rstd * gains[0]

    def norm(k, carry):
        rows = pl.ds(pl.multiple_of(k * 208, 16), 208)
        nb[rows, :] = ((x32[rows, :] - mean) * scale).astype(BF16)
        return carry

    lax.fori_loop(0, 4, norm, 0)

    def attend(k, carry):
        total, square = carry
        rows = pl.ds(pl.multiple_of(k * 208, 16), 208)
        q = dot(nb[rows, :], wm[...]).astype(BF16)
        s = dot_t(q, nb[...])
        p = jnp.exp2(s - jnp.max(s, axis=1, keepdims=True))
        bottom = jnp.sum(p, axis=1, keepdims=True)
        context = (dot(p.astype(BF16), nb[...]) / bottom).astype(BF16)
        v = (x32[rows, :] + dot(context, wn[...])).astype(BF16).astype(F32)
        x32[rows, :] = v
        return (
            total + jnp.sum(v, axis=0, keepdims=True),
            square + jnp.sum(v * v, axis=0, keepdims=True),
        )

    mean, rstd = wide_moments(*lax.fori_loop(0, 4, attend, (zero, zero)))
    scale1 = rstd * gains[1]

    def activate(k, carry):
        rows = pl.ds(pl.multiple_of(k * 208, 16), 208)
        act[rows, :] = silu((x32[rows, :] - mean) * scale1).astype(BF16)
        return carry

    lax.fori_loop(0, 4, activate, 0)

    def fx(src, dst, there, k, slot):
        return pltpu.make_async_remote_copy(
            src_ref=src,
            dst_ref=dst,
            send_sem=fx_send.at[k],
            recv_sem=fx_recv.at[slot],
            device_id={"tm": there},
            device_id_type=MESH,
        )

    def columns(first, last):
        def one(k, carry):
            cols = pl.ds(pl.multiple_of(k * 256, 256), 256)
            zs[:, cols] = dot(act[...], w1t[:, cols])
            return carry

        lax.fori_loop(first, last, one, 0)
        if last == 6:
            zs[:, 1536:1728] = dot(act[...], w1t[:, 1536:1728])

    def fold(time):
        first, last, half = FIRST_PLACES[time]
        z = lambda c, n=128: zs[:, c : c + n].reshape(ROWS, COLS, n)
        low = lane_low((ROWS, COLS, 128))
        shifted = col_before_after(
            row_before(z(first)) + z(first + 128) + row_after(z(first + 256))
        )
        middle = z(first + 384)
        middle = jnp.where(low, row_before(middle), middle)
        if time < 2:
            extra = row_after(z(last))
        else:
            extra = jnp.concatenate(
                [row_after(z(last, 64)), jnp.zeros((ROWS, COLS, 64), F32)], axis=2
            )
        extra = jnp.where(low if half == 0 else ~low, extra, 0.0)
        total = shifted + middle + extra
        total = total + pltpu.roll(total, 64, 2)
        packed = jnp.where(low[0:4], total[0:4], total[4:8])
        return packed.reshape(CELLS // 2, 128)

    columns(0, 3)
    msg[0] = fold(0).astype(BF16)

    @pl.when(t < frames - 2)
    def _():
        fx(msg.at[0], in1.at[1], t + 2, 0, 1).start()

    @pl.when(t == 0)
    def _():
        fx(msg.at[0], in1.at[1], t + 1, 1, 1).start()
        in1[1] = msg[0]

    columns(3, 5)
    msg[1] = fold(1).astype(BF16)

    @pl.when(t < frames - 1)
    def _():
        fx(msg.at[1], in1.at[0], t + 1, 2, 0).start()

    @pl.when(t == 0)
    def _():
        in1[0] = msg[1]

    columns(5, 6)
    hidden = fold(2)

    @pl.when(t >= 1)
    def _():
        fx(msg.at[0], in1.at[1], t, 0, 1).wait_recv()
        fx(msg.at[1], in1.at[0], t, 2, 0).wait_recv()

    hidden = hidden + in1[0].astype(F32) + in1[1].astype(F32)

    pieces = [
        jnp.sum(hidden, axis=0, keepdims=True),
        jnp.sum(hidden * hidden, axis=0, keepdims=True),
        jnp.zeros((6, 128), F32),
    ]
    mean, rstd = moments(jnp.concatenate(pieces, axis=0), 64, CELLS * WIDTH, 1)
    gain = jnp.concatenate([gain2v[...], gain2v[...]], axis=1)
    u = silu((hidden - mean) * (rstd * gain)).astype(BF16)
    ua[...] = u

    @pl.when(t < frames - 1)
    def _():
        fx(ua, in2.at[0], t + 1, 3, 2).start()

    @pl.when(t < frames - 2)
    def _():
        fx(ua, in2.at[1], t + 2, 4, 3).start()

    @pl.when(t == 0)
    def _():
        fx(ua, in2.at[1], t + 1, 5, 3).start()
        in2[0] = ua[...]
        in2[1] = ua[...]

    def spread(dense):
        d = dense.astype(F32).reshape(4, COLS, 128)
        low = lane_low((4, COLS, 128))
        other = pltpu.roll(d, 64, 2)
        both = jnp.concatenate([jnp.where(low, d, other), jnp.where(low, other, d)], axis=0)
        sides = col_before_after(both)
        flat = lambda v: v.reshape(CELLS, 128)
        wide = [
            flat(row_before(sides)),
            flat(sides),
            flat(row_after(sides)),
            flat(jnp.where(lane_low(both.shape), row_before(both), both)),
        ]
        return wide, flat(row_after(both))

    pltpu.make_async_copy(w2, w2, load_sem.at[10]).wait()
    wide, last2 = spread(u)
    for k in range(4):
        xown[:, 128 * k : 128 * k + 128] = wide[k].astype(BF16)
    xrest[:, 1152:1216] = last2[:, 0:64].astype(BF16)

    def mine(k, carry):
        cols = pl.ds(pl.multiple_of(k * 256, 256), 256)
        acc[:, cols] = dot(xown[...], w2[0:512, cols])
        return carry

    lax.fori_loop(0, 2, mine, 0)

    @pl.when(t >= 1)
    def _():
        fx(ua, in2.at[0], t, 3, 2).wait_recv()

    wide, last1 = spread(in2[0])
    for k in range(4):
        xrest[:, 128 * k : 128 * k + 128] = wide[k].astype(BF16)

    @pl.when(t >= 1)
    def _():
        fx(ua, in2.at[1], t, 4, 3).wait_recv()

    wide, last0 = spread(in2[1])
    for k in range(4):
        xrest[:, 512 + 128 * k : 640 + 128 * k] = wide[k].astype(BF16)
    xrest[:, 1024:1152] = jnp.where(lane_low(last0.shape), last1, last0).astype(BF16)

    def partial_sums(where):
        rows = pl.ds(pl.multiple_of(where * 208, 16), 208)
        acc[rows, :] = acc[rows, :] + dot(xrest[rows, :], w2[512:1728, :])

    def piece(where, hh, half):
        rows = pl.ds(pl.multiple_of(where * 208 + hh * COLS, 8), COLS)
        return acc[rows, HALF * half : HALF * half + HALF]

    sent = []

    def rs_go(src, dst, there, recv):
        c = pltpu.make_async_remote_copy(
            src_ref=src,
            dst_ref=dst,
            send_sem=rs_send.at[len(sent)],
            recv_sem=rs_recv.at[recv],
            device_id={"tok": there},
            device_id_type=MESH,
        )
        c.start()
        sent.append(c)

    def rs_wait(dst, recv):
        pltpu.make_async_remote_copy(
            src_ref=dst,
            dst_ref=dst,
            send_sem=rs_send.at[0],
            recv_sem=rs_recv.at[recv],
            device_id={"tok": across},
            device_id_type=MESH,
        ).wait_recv()

    sides = (o, h)
    partial_sums(y2)
    for r in range(2):
        for half, there in ((0, up), (1, down)):
            rs1s[r, half] = piece(y2, sides[r], half).astype(BF16)
            rs_go(rs1s.at[r, half], rs1r.at[r, half], there, 2 * r + half)

    partial_sums(yp)
    for r in range(2):
        rs2s[r, 0, 1] = piece(yp, sides[r], 1).astype(BF16)
        rs_go(rs2s.at[r, 0, 1], rs2r.at[r, 0, 1], up, 4 + 4 * r + 1)
    partial_sums(ym)
    for r in range(2):
        rs2s[r, 1, 0] = piece(ym, sides[r], 0).astype(BF16)
        rs_go(rs2s.at[r, 1, 0], rs2r.at[r, 1, 0], down, 4 + 4 * r + 2)
    for r in range(2):
        rs_wait(rs1r.at[r, 0], 2 * r)
        rs2s[r, 0, 0] = (piece(yp, sides[r], 0) + rs1r[r, 0].astype(F32)).astype(BF16)
        rs_go(rs2s.at[r, 0, 0], rs2r.at[r, 0, 0], up, 4 + 4 * r)
        rs_wait(rs1r.at[r, 1], 2 * r + 1)
        rs2s[r, 1, 1] = (piece(ym, sides[r], 1) + rs1r[r, 1].astype(F32)).astype(BF16)
        rs_go(rs2s.at[r, 1, 1], rs2r.at[r, 1, 1], down, 4 + 4 * r + 3)
    partial_sums(y)

    def summed(r, half):
        for d in range(2):
            rs_wait(rs2r.at[r, d, half], 4 + 4 * r + 2 * d + half)
        return (
            piece(y, sides[r], half)
            + rs2r[r, 0, half].astype(F32)
            + rs2r[r, 1, half].astype(F32)
        )

    for half in (1, 0):
        zsend[half] = summed(0, half).astype(BF16)
        rs_go(zsend.at[half], zrecv.at[half], across, 12 + half)
    mine_rows = pl.ds(pl.multiple_of(me * COLS, 8), COLS)
    for half in (1, 0):
        cols = slice(HALF * half, HALF * half + HALF)
        v = summed(1, half) + x32[mine_rows, cols]
        rs_wait(zrecv.at[half], 12 + half)
        out[0, :, cols] = (v + zrecv[half].astype(F32)).astype(BF16)

    for c in gathered + sent:
        c.wait_send()

    @pl.when(t < frames - 2)
    def _():
        fx(msg.at[0], in1.at[1], t, 0, 1).wait_send()
        fx(ua, in2.at[1], t, 4, 3).wait_send()

    @pl.when(t < frames - 1)
    def _():
        fx(msg.at[1], in1.at[0], t, 2, 0).wait_send()
        fx(ua, in2.at[0], t, 3, 2).wait_send()

    @pl.when(t == 0)
    def _():
        fx(msg.at[0], in1.at[1], t, 1, 1).wait_send()
        fx(ua, in2.at[1], t, 5, 3).wait_send()


def per_device(tokens, gain0, wq, wk, wv, wo, gain1, k1, gain2, k2):
    dma = pltpu.SemaphoreType.DMA
    vmem = pltpu.VMEM
    return pl.pallas_call(
        kernel,
        out_shape=jax.ShapeDtypeStruct((1, COLS, C), BF16),
        in_specs=[pl.BlockSpec(memory_space=pl.ANY)] * 10,
        out_specs=pl.BlockSpec(memory_space=pltpu.VMEM),
        scratch_shapes=[
            vmem((ROWS, 2, COLS, HALF), BF16),
            vmem((CELLS, C), F32),
            vmem((CELLS, C), BF16),
            vmem((4, C, C), BF16),
            vmem((C, C), BF16),
            vmem((C, C), BF16),
            vmem((27 * LOCAL, C), BF16),
            vmem((C, 27 * LOCAL), BF16),
            vmem((27 * LOCAL, C), BF16),
            vmem((2, 1, C), F32),
            vmem((1, LOCAL), F32),
            vmem((CELLS, C), BF16),
            vmem((CELLS, 27 * LOCAL), F32),
            vmem((2, CELLS // 2, 128), BF16),
            vmem((CELLS, C), F32),
            vmem((CELLS, C), BF16),
            vmem((CELLS, 19 * LOCAL), BF16),
            vmem((CELLS // 2, 128), BF16),
            vmem((2, CELLS // 2, 128), BF16),
            vmem((2, CELLS // 2, 128), BF16),
            vmem((2, 2, COLS, HALF), BF16),
            vmem((2, 2, COLS, HALF), BF16),
            vmem((2, 2, 2, COLS, HALF), BF16),
            vmem((2, 2, 2, COLS, HALF), BF16),
            vmem((2, COLS, HALF), BF16),
            vmem((2, COLS, HALF), BF16),
            dma((11,)),
            dma((14,)),
            dma((ROWS, 2)),
            dma((6,)),
            dma((4,)),
            dma((14,)),
            dma((14,)),
        ],
        compiler_params=pltpu.CompilerParams(
            collective_id=0, has_side_effects=True, vmem_limit_bytes=56 * 2**20
        ),
    )(
        tokens,
        gain0.reshape(1, C),
        wq,
        wk,
        wv,
        wo,
        gain1.reshape(1, C),
        jnp.swapaxes(k1, 3, 4),
        gain2.reshape(1, LOCAL),
        k2,
    )


def solution(mesh):
    placed = (
        P("tm", "tok", None),
        P(),
        P(),
        P(),
        P(),
        P(),
        P(),
        P(None, None, None, None, "tok"),
        P("tok"),
        P(None, None, None, "tok", None),
    )
    return jax.shard_map(
        per_device, mesh=mesh, in_specs=placed, out_specs=P("tm", "tok", None), check_vma=False
    )
```

```python
import math

import jax
import jax.numpy as jnp
from jax import lax
from jax.experimental import pallas as pl
from jax.experimental.pallas import tpu as pltpu
from jax.sharding import PartitionSpec as P

F32 = jnp.float32
BF16 = jnp.bfloat16
MESH = pl.DeviceIdType.MESH

C = 512
HALF = C // 2
ROWS = 8
COLS = 104
CELLS = ROWS * COLS
WIDTH = 16
LOCAL = 64
EPSILON = 1e-06

ORDER = (0, 2, 4, 6, 1, 3, 5, 7)

PAIRS = ((0, 0), (0, 2), (1, 0), (1, 2), (2, 0), (2, 2), (0, 1), (1, 1))
LAST = (2, 1)


def taps_of(time):
    return tuple((time,) + pair for pair in PAIRS)


FIRST_ORDER = (
    taps_of(0) + ((0,) + LAST, (1,) + LAST) + taps_of(1) + taps_of(2) + ((2,) + LAST,)
)
SECOND_ORDER = (
    taps_of(2) + taps_of(1) + taps_of(0) + ((1,) + LAST, (0,) + LAST, (2,) + LAST)
)
FIRST_PLACES = ((0, 512, 0), (640, 512, 1), (1152, 1664, 0))


def lane_low(shape):
    return lax.broadcasted_iota(jnp.int32, shape, len(shape) - 1) < 64


def row_before(x):
    return jnp.concatenate([x[0:1], x[0 : ROWS - 1]], axis=0)


def row_after(x):
    return jnp.concatenate([x[1:ROWS], x[ROWS - 1 : ROWS]], axis=0)


def col_before_after(x):
    col = lax.broadcasted_iota(jnp.int32, x.shape, 1)
    before = jnp.where(col == 0, x, pltpu.roll(x, 1, 1))
    after = jnp.where(col == COLS - 1, x, pltpu.roll(x, COLS - 1, 1))
    return jnp.where(lane_low(x.shape), before, after)


def group_matrix(period):
    i = lax.broadcasted_iota(jnp.int32, (128, 128), 0)
    k = lax.broadcasted_iota(jnp.int32, (128, 128), 1)
    same = ((i & (period - 1)) >> 4) == ((k & (period - 1)) >> 4)
    return jnp.where(same, 1.0, 0.0).astype(F32)


def moments(stacked, period, entries, n):
    totals = (
        jnp.dot(
            stacked,
            group_matrix(period),
            precision=lax.Precision.HIGHEST,
            preferred_element_type=F32,
        )
        / entries
    )
    mean = totals[0:n]
    var = totals[n : 2 * n] - mean * mean
    return mean, lax.rsqrt(var + EPSILON)


def wide_moments(total, square):
    pieces = [total[:, 128 * k : 128 * k + 128] for k in range(4)]
    pieces += [square[:, 128 * k : 128 * k + 128] for k in range(4)]
    mean, rstd = moments(jnp.concatenate(pieces, axis=0), 128, CELLS * WIDTH, 4)
    spread = lambda v: jnp.concatenate([v[k : k + 1] for k in range(4)], axis=1)
    return spread(mean), spread(rstd)


def silu(v):
    return v * (0.5 * jnp.tanh(0.5 * v) + 0.5)


def dot(a, b):
    return jnp.dot(a, b, preferred_element_type=F32)


def dot_t(a, b):
    return lax.dot_general(a, b, (((1,), (1,)), ((), ())), preferred_element_type=F32)


def kernel(
    tok, gain0, wq, wk, wv, wo, gain1, k1, gain2, k2, out,
    stage, xg, x32, nb, wts, wm, wn, w1r, w1t, w2, gains, gain2v, act, zs, sums, hid, msg, acc,
    xown, xrest, ua, in1, in2, rss, rsr, zsend, zrecv, zdirect, near,
    load_sem, ag_send, ag_recv, fx_send, fx_recv, rs_send, rs_recv, z_send, z_recv, zd_send, zd_recv,
):
    me = lax.axis_index("tok")
    t = lax.axis_index("tm")
    frames = lax.axis_size("tm")
    y = me // 2
    h = me % 2
    o = 1 - h
    across = 2 * y + o

    def worker(frame):
        plane, place = frame // 8, frame % 8
        turned = 8 * plane + 2 * (3 - place // 2) + place % 2
        return jnp.where(plane % 2 == 1, turned, frame)

    f = worker(t)
    odd = (t // 8) % 2 == 1
    even = (t // 8) % 2 == 0
    middle = (t // 2) % 4
    outer = jnp.logical_and(odd, middle % 3 == 0)
    far = jnp.where(outer, h, o)
    close = 1 - far
    y2 = (y + 2) % 4
    beyond = 2 * y2 + far

    def beside(d):
        return 2 * ((y + d) % 4) + h

    dma = pltpu.make_async_copy

    own = [
        dma(tok.at[0, :, pl.ds(HALF * k, HALF)], stage.at[k], load_sem.at[k]) for k in range(2)
    ]
    kept = [
        dma(tok.at[0, :, pl.ds(HALF * k, HALF)], xg.at[me, k], load_sem.at[11 + k])
        for k in range(2)
    ]
    small = [
        dma(gain0, gains.at[0], load_sem.at[2]),
        dma(gain1, gains.at[1], load_sem.at[3]),
        dma(gain2, gain2v, load_sem.at[4]),
    ]
    mats = [dma(w, wts.at[k], load_sem.at[5 + k]) for k, w in enumerate((wq, wk, wv, wo))]
    barrier = pltpu.get_barrier_semaphore()

    def greet(**there):
        pl.semaphore_signal(barrier, inc=1, device_id=there, device_id_type=MESH)

    def load():
        for c in own:
            c.start()

        @pl.when(even)
        def _():
            for c in kept:
                c.start()

        @pl.when(even)
        def _():
            greet(tok=across)

        @pl.when(odd)
        def _():
            greet(tm=f, tok=across)
            greet(tm=f, tok=me)

        greet(tm=f, tok=beyond)
        for d in (2, 1, 3):
            greet(tok=beside(d))

        @pl.when(f >= 1)
        def _():
            greet(tm=worker(f - 1))

        @pl.when(f >= 2)
        def _():
            greet(tm=worker(f - 2))

    def all_entered():
        for c in own:
            c.wait()
        late = jnp.where(f < frames - 1, 1, 0) + jnp.where(f < frames - 2, 1, 0)
        pl.semaphore_wait(barrier, 5 + jnp.where(odd, 1, 0) + late)

    def load_weights():
        for c in mats + small:
            c.start()
        for k, (a, b, e) in enumerate(FIRST_ORDER):
            dma(k1.at[a, b, e], w1r.at[pl.ds(LOCAL * k, LOCAL)], load_sem.at[9]).start()
        for k, (a, b, e) in enumerate(SECOND_ORDER):
            dma(k2.at[a, b, e], w2.at[pl.ds(LOCAL * k, LOCAL)], load_sem.at[10]).start()

    def ag(src, block, half, k, **there):
        return pltpu.make_async_remote_copy(
            src_ref=src,
            dst_ref=xg.at[block, half],
            send_sem=ag_send.at[k],
            recv_sem=ag_recv.at[block, half],
            device_id=there,
            device_id_type=MESH,
        )

    def ag_wait(block, half):
        ag(stage.at[0], block, half, 0, tok=across).wait_recv()

    def own_send(half, k):
        there = (2 * y + far, beyond, 2 * y + close)[k]
        return ag(stage.at[half], 2 * y + h, half, 3 * half + k, tm=f, tok=there)

    def gather_own():
        for half in range(2):
            own_send(half, 0).start()

            @pl.when(odd)
            def _():
                own_send(half, 2).start()

        for half in range(2):
            own_send(half, 1).start()

    gathered = []

    def gather_side(side, first):
        block = 2 * y + side
        for half in range(2):
            if first:

                @pl.when(even)
                def _():
                    kept[half].wait()

                @pl.when(odd)
                def _():
                    ag_wait(block, half)

            else:
                ag_wait(block, half)
            for d in (2, 1, 3) if first else (1, 3):
                c = ag(xg.at[block, half], block, half, 6 + len(gathered), tok=beside(d))
                c.start()
                gathered.append(c)

    counted = [jnp.zeros((8, C), F32), jnp.zeros((8, C), F32)]

    def collect(block):
        v = jnp.concatenate([xg[block, 0].astype(F32), xg[block, 1].astype(F32)], axis=1)
        x32[pl.ds(pl.multiple_of(block * COLS, 8), COLS), :] = v
        v = v.reshape(COLS // 8, 8, C)
        counted[0] = counted[0] + jnp.sum(v, axis=0)
        counted[1] = counted[1] + jnp.sum(v * v, axis=0)

    def collect_side(side, ds, here):
        if here:
            collect(2 * y + side)
        for d in ds:
            block = 2 * ((y + d) % 4) + side
            for half in range(2):
                ag_wait(block, half)
            collect(block)

    def fold_scores():
        for c in mats[:2]:
            c.wait()
        wm[...] = (dot_t(wts[0], wts[1]) * (math.log2(math.e) / math.sqrt(C))).astype(BF16)

    def fold_values():
        for c in mats[2:]:
            c.wait()
        wn[...] = dot(wts[2], wts[3]).astype(BF16)

    def turn_first():
        dma(w1r, w1r, load_sem.at[9]).wait()
        w1t[...] = w1r[...].T

    def norm_tokens():
        for c in small:
            c.wait()

        total, square = (jnp.sum(v, axis=0, keepdims=True) for v in counted)
        mean, rstd = wide_moments(total, square)
        scale = rstd * gains[0]

        def norm(k, carry):
            rows = pl.ds(pl.multiple_of(k * 208, 16), 208)
            nb[rows, :] = ((x32[rows, :] - mean) * scale).astype(BF16)
            return carry

        lax.fori_loop(0, 4, norm, 0)

    def attention():
        q = dot(nb[...], wm[...]).astype(BF16)
        s = dot_t(q, nb[...])
        p = jnp.exp2(s - jnp.max(s, axis=1, keepdims=True))
        bottom = jnp.sum(p, axis=1, keepdims=True)
        context = (dot(p.astype(BF16), nb[...]) / bottom).astype(BF16)
        v = (x32[...] + dot(context, wn[...])).astype(BF16).astype(F32)
        x32[...] = v
        sums[0] = jnp.sum(v, axis=0, keepdims=True)
        sums[1] = jnp.sum(v * v, axis=0, keepdims=True)

    def activate():
        mean, rstd = wide_moments(sums[0], sums[1])
        scale = rstd * gains[1]

        def one(k, carry):
            rows = pl.ds(pl.multiple_of(k * 208, 16), 208)
            act[rows, :] = silu((x32[rows, :] - mean) * scale).astype(BF16)
            return carry

        lax.fori_loop(0, 4, one, 0)

    def fx(src, dst, there, k, slot):
        return pltpu.make_async_remote_copy(
            src_ref=src,
            dst_ref=dst,
            send_sem=fx_send.at[k],
            recv_sem=fx_recv.at[slot],
            device_id={"tm": there},
            device_id_type=MESH,
        )

    def columns(first, last):
        cols = slice(256 * first, min(256 * last, 27 * LOCAL))
        zs[:, cols] = dot(act[...], w1t[:, cols])

    def fold(time):
        first, last, half = FIRST_PLACES[time]
        z = lambda c, n=128: zs[:, c : c + n].reshape(ROWS, COLS, n)
        low = lane_low((ROWS, COLS, 128))
        shifted = col_before_after(
            row_before(z(first)) + z(first + 128) + row_after(z(first + 256))
        )
        middle = z(first + 384)
        middle = jnp.where(low, row_before(middle), middle)
        if time < 2:
            extra = row_after(z(last))
        else:
            extra = jnp.concatenate(
                [row_after(z(last, 64)), jnp.zeros((ROWS, COLS, 64), F32)], axis=2
            )
        extra = jnp.where(low if half == 0 else ~low, extra, 0.0)
        total = shifted + middle + extra
        total = total + pltpu.roll(total, 64, 2)
        packed = jnp.where(low[0:4], total[0:4], total[4:8])
        return packed.reshape(CELLS // 2, 128)

    def first_two_ahead():
        columns(0, 3)
        msg[0] = fold(0).astype(BF16)

    def send_two_ahead():
        @pl.when(f < frames - 2)
        def _():
            fx(msg.at[0], in1.at[1], worker(f + 2), 0, 1).start()

        @pl.when(f == 0)
        def _():
            fx(msg.at[0], in1.at[1], worker(f + 1), 1, 1).start()
            in1[1] = msg[0]

    def first_one_ahead():
        columns(3, 5)
        msg[1] = fold(1).astype(BF16)

    def send_one_ahead():
        @pl.when(f < frames - 1)
        def _():
            fx(msg.at[1], in1.at[0], worker(f + 1), 2, 0).start()

        @pl.when(f == 0)
        def _():
            in1[0] = msg[1]

    def first_own():
        columns(5, 7)
        hid[...] = fold(2)

    def wait_first():
        @pl.when(f >= 1)
        def _():
            fx(msg.at[0], in1.at[1], f, 0, 1).wait_recv()
            fx(msg.at[1], in1.at[0], f, 2, 0).wait_recv()

    def activate_second():
        hidden = hid[...] + in1[0].astype(F32) + in1[1].astype(F32)
        pieces = [
            jnp.sum(hidden, axis=0, keepdims=True),
            jnp.sum(hidden * hidden, axis=0, keepdims=True),
            jnp.zeros((6, 128), F32),
        ]
        mean, rstd = moments(jnp.concatenate(pieces, axis=0), 64, CELLS * WIDTH, 1)
        gain = jnp.concatenate([gain2v[...], gain2v[...]], axis=1)
        ua[...] = silu((hidden - mean) * (rstd * gain)).astype(BF16)

    def send_second():
        @pl.when(f < frames - 1)
        def _():
            fx(ua, in2.at[0], worker(f + 1), 3, 2).start()

        @pl.when(f < frames - 2)
        def _():
            fx(ua, in2.at[1], worker(f + 2), 4, 3).start()

        @pl.when(f == 0)
        def _():
            fx(ua, in2.at[1], worker(f + 1), 5, 3).start()
            in2[0] = ua[...]
            in2[1] = ua[...]

    def spread(dense):
        d = dense.astype(F32).reshape(4, COLS, 128)
        low = lane_low((4, COLS, 128))
        other = pltpu.roll(d, 64, 2)
        both = jnp.concatenate([jnp.where(low, d, other), jnp.where(low, other, d)], axis=0)
        sides = col_before_after(both)
        flat = lambda v: jnp.concatenate([v[r : r + 1] for r in ORDER], axis=0).reshape(CELLS, 128)
        wide = [
            flat(row_before(sides)),
            flat(sides),
            flat(row_after(sides)),
            flat(jnp.where(lane_low(both.shape), row_before(both), both)),
        ]
        return wide, flat(row_after(both))

    def second_own():
        dma(w2, w2, load_sem.at[10]).wait()
        wide, last = spread(ua[...])
        for k in range(4):
            xown[:, 128 * k : 128 * k + 128] = wide[k].astype(BF16)
        xrest[:, 1152:1216] = last[:, 0:64].astype(BF16)

        acc[...] = dot(xown[...], w2[0:512, :])

    def wait_second(back):
        @pl.when(f >= 1)
        def _():
            fx(ua, in2.at[back], f, 3 + back, 2 + back).wait_recv()

    def second_back():
        wide, last1 = spread(in2[0])
        for k in range(4):
            xrest[:, 128 * k : 128 * k + 128] = wide[k].astype(BF16)
        wait_second(1)
        wide, last0 = spread(in2[1])
        for k in range(4):
            xrest[:, 512 + 128 * k : 640 + 128 * k] = wide[k].astype(BF16)
        xrest[:, 1024:1152] = jnp.where(lane_low(last0.shape), last1, last0).astype(BF16)

    half_frame = CELLS // 2
    scattered = []

    def rs(r, half, d):
        return pltpu.make_async_remote_copy(
            src_ref=rss.at[r, half, (y + d) % 4],
            dst_ref=rsr.at[r, half, d - 1],
            send_sem=rs_send.at[r, half, d - 1],
            recv_sem=rs_recv.at[r, half, d - 1],
            device_id={"tok": beside(d)},
            device_id_type=MESH,
        )

    def sum_rows(r, side, half):
        rows = pl.ds(pl.multiple_of(side * half_frame, 16), half_frame)
        cols = slice(HALF * half, HALF * half + HALF)
        v = acc[rows, cols] + dot(xrest[rows, :], w2[512:1728, cols])
        acc[rows, cols] = v
        rss[r, half] = v.reshape(4, COLS, HALF).astype(BF16)

    def direct(half):
        return pltpu.make_async_remote_copy(
            src_ref=rss.at[0, half, y2],
            dst_ref=zdirect.at[half],
            send_sem=zd_send.at[half],
            recv_sem=zd_recv.at[half],
            device_id={"tm": f, "tok": beyond},
            device_id_type=MESH,
        )

    def send_rows(r, half):
        for d in (1, 3) if r == 0 else (2, 1, 3):
            c = rs(r, half, d)
            c.start()
            scattered.append(c)
        if r == 0:
            c = direct(half)
            c.start()
            scattered.append(c)

    def home(r, side, half):
        return pltpu.make_async_remote_copy(
            src_ref=zsend.at[r, half],
            dst_ref=zrecv.at[h, half],
            send_sem=z_send.at[r, half],
            recv_sem=z_recv.at[h, half],
            device_id={"tm": f, "tok": 2 * y + side},
            device_id_type=MESH,
        )

    def collect_rows(r, side, half):
        come = (1, 3) if r == 0 else (1, 3, 2)
        for d in come:
            rs(r, half, d).wait_recv()
        rows = pl.ds(pl.multiple_of(side * half_frame + y * COLS, 8), COLS)
        cols = slice(HALF * half, HALF * half + HALF)
        v = acc[rows, cols]
        for d in come:
            v = v + rsr[r, half, d - 1].astype(F32)
        own_rows = pl.ds(pl.multiple_of(me * COLS, 8), COLS)
        v = v + jnp.where(side == h, x32[own_rows, cols], 0.0)
        return v

    def scatter():
        for r, side in ((0, far), (1, close)):
            for half in range(2):
                sum_rows(r, side, half)
                send_rows(r, half)
        for half in range(2):
            zsend[0, half] = collect_rows(0, far, half).astype(BF16)
            home(0, far, half).start()
        for half in range(2):
            v = collect_rows(1, close, half)

            @pl.when(even)
            def _():
                near[half] = v

            @pl.when(odd)
            def _():
                zsend[1, half] = v.astype(BF16)
                home(1, close, half).start()

    def home_wait(source, half):
        pltpu.make_async_remote_copy(
            src_ref=zsend.at[0, half],
            dst_ref=zrecv.at[source, half],
            send_sem=z_send.at[0, half],
            recv_sem=z_recv.at[source, half],
            device_id={"tok": across},
            device_id_type=MESH,
        ).wait_recv()

    def last():
        for half in range(2):
            cols = slice(HALF * half, HALF * half + HALF)

            @pl.when(odd)
            def _():
                home_wait(h, half)
                near[half] = zrecv[h, half].astype(F32)

            direct(half).wait_recv()
            v = near[half] + zdirect[half].astype(F32)
            home_wait(o, half)
            out[0, :, cols] = (v + zrecv[o, half].astype(F32)).astype(BF16)

    def finish():
        for c in gathered + scattered:
            c.wait_send()
        for half in range(2):
            own_send(half, 0).wait_send()
            own_send(half, 1).wait_send()

            @pl.when(odd)
            def _():
                own_send(half, 2).wait_send()

    def finish_home():
        for half in range(2):
            home(0, far, half).wait_send()

            @pl.when(odd)
            def _():
                home(1, close, half).wait_send()

    def finish_frames():
        @pl.when(f < frames - 2)
        def _():
            fx(msg.at[0], in1.at[1], f, 0, 1).wait_send()
            fx(ua, in2.at[1], f, 4, 3).wait_send()

        @pl.when(f < frames - 1)
        def _():
            fx(msg.at[1], in1.at[0], f, 2, 0).wait_send()
            fx(ua, in2.at[0], f, 3, 2).wait_send()

        @pl.when(f == 0)
        def _():
            fx(msg.at[0], in1.at[1], f, 1, 1).wait_send()
            fx(ua, in2.at[1], f, 5, 3).wait_send()

    load()
    all_entered()
    gather_own()
    load_weights()
    gather_side(close, True)
    fold_scores()
    fold_values()
    collect_side(close, (1, 3), True)
    gather_side(far, False)
    turn_first()
    collect_side(close, (2,), False)
    collect_side(far, (1, 3, 2), True)
    norm_tokens()
    attention()
    activate()
    first_two_ahead()
    send_two_ahead()
    first_one_ahead()
    send_one_ahead()
    first_own()
    wait_first()
    activate_second()
    send_second()
    second_own()
    wait_second(0)
    second_back()
    scatter()
    last()
    finish()
    finish_home()
    finish_frames()


def per_device(tokens, gain0, wq, wk, wv, wo, gain1, k1, gain2, k2):
    dma = pltpu.SemaphoreType.DMA
    vmem = pltpu.VMEM
    return pl.pallas_call(
        kernel,
        out_shape=pltpu.VMEM((1, COLS, C), BF16),
        in_specs=[pl.BlockSpec(memory_space=pl.ANY)] * 10,
        out_specs=pl.BlockSpec(memory_space=pltpu.VMEM),
        scratch_shapes=[
            vmem((2, COLS, HALF), BF16),
            vmem((ROWS, 2, COLS, HALF), BF16),
            vmem((CELLS, C), F32),
            vmem((CELLS, C), BF16),
            vmem((4, C, C), BF16),
            vmem((C, C), BF16),
            vmem((C, C), BF16),
            vmem((27 * LOCAL, C), BF16),
            vmem((C, 27 * LOCAL), BF16),
            vmem((27 * LOCAL, C), BF16),
            vmem((2, 1, C), F32),
            vmem((1, LOCAL), F32),
            vmem((CELLS, C), BF16),
            vmem((CELLS, 27 * LOCAL), F32),
            vmem((2, 1, C), F32),
            vmem((CELLS // 2, 128), F32),
            vmem((2, CELLS // 2, 128), BF16),
            vmem((CELLS, C), F32),
            vmem((CELLS, C), BF16),
            vmem((CELLS, 19 * LOCAL), BF16),
            vmem((CELLS // 2, 128), BF16),
            vmem((2, CELLS // 2, 128), BF16),
            vmem((2, CELLS // 2, 128), BF16),
            vmem((2, 2, 4, COLS, HALF), BF16),
            vmem((2, 2, 3, COLS, HALF), BF16),
            vmem((2, 2, COLS, HALF), BF16),
            vmem((2, 2, COLS, HALF), BF16),
            vmem((2, COLS, HALF), BF16),
            vmem((2, COLS, HALF), F32),
            dma((13,)),
            dma((16,)),
            dma((ROWS, 2)),
            dma((6,)),
            dma((4,)),
            dma((2, 2, 3)),
            dma((2, 2, 3)),
            dma((2, 2)),
            dma((2, 2)),
            dma((2,)),
            dma((2,)),
        ],
        compiler_params=pltpu.CompilerParams(
            collective_id=0, has_side_effects=True, vmem_limit_bytes=56 * 2**20
        ),
    )(
        tokens,
        gain0.reshape(1, C),
        wq,
        wk,
        wv,
        wo,
        gain1.reshape(1, C),
        jnp.swapaxes(k1, 3, 4),
        gain2.reshape(1, LOCAL),
        k2,
    )


def solution(mesh):
    placed = (
        P("tm", "tok", None),
        P(),
        P(),
        P(),
        P(),
        P(),
        P(),
        P(None, None, None, None, "tok"),
        P("tok"),
        P(None, None, None, "tok", None),
    )
    return jax.shard_map(
        per_device, mesh=mesh, in_specs=placed, out_specs=P("tm", "tok", None), check_vma=False
    )
```

```python
import math

import jax
import jax.numpy as jnp
from jax import lax
from jax.experimental import pallas as pl
from jax.experimental.pallas import tpu as pltpu
from jax.sharding import PartitionSpec as P

F32 = jnp.float32
BF16 = jnp.bfloat16
MESH = pl.DeviceIdType.MESH

C = 512
PIECES = 2
PIECE = C // PIECES
PARTS = 2
PART = C // PARTS
ROWS = 8
COLS = 104
CELLS = ROWS * COLS
WIDTH = 16
LOCAL = 64
EPSILON = 1e-06

ORDER = (0, 2, 4, 6, 1, 3, 5, 7)

PAIRS = ((0, 0), (0, 2), (1, 0), (1, 2), (2, 0), (2, 2), (0, 1), (1, 1))
LAST = (2, 1)


def taps_of(time):
    return tuple((time,) + pair for pair in PAIRS)


FIRST_ORDER = (
    taps_of(0) + ((0,) + LAST, (1,) + LAST) + taps_of(1) + taps_of(2) + ((2,) + LAST,)
)
SECOND_ORDER = (
    taps_of(2) + taps_of(0) + taps_of(1) + ((1,) + LAST, (0,) + LAST, (2,) + LAST)
)
FIRST_PLACES = ((0, 512, 0), (640, 512, 1), (1152, 1664, 0))


def lane_low(shape):
    return lax.broadcasted_iota(jnp.int32, shape, len(shape) - 1) < 64


def row_before(x):
    return jnp.concatenate([x[0:1], x[0 : ROWS - 1]], axis=0)


def row_after(x):
    return jnp.concatenate([x[1:ROWS], x[ROWS - 1 : ROWS]], axis=0)


def col_before_after(x):
    col = lax.broadcasted_iota(jnp.int32, x.shape, 1)
    before = jnp.where(col == 0, x, pltpu.roll(x, 1, 1))
    after = jnp.where(col == COLS - 1, x, pltpu.roll(x, COLS - 1, 1))
    return jnp.where(lane_low(x.shape), before, after)


def group_matrix(period):
    i = lax.broadcasted_iota(jnp.int32, (128, 128), 0)
    k = lax.broadcasted_iota(jnp.int32, (128, 128), 1)
    same = ((i & (period - 1)) >> 4) == ((k & (period - 1)) >> 4)
    return jnp.where(same, 1.0, 0.0).astype(F32)


def moments(stacked, period, entries, n):
    totals = (
        jnp.dot(
            stacked,
            group_matrix(period),
            precision=lax.Precision.HIGHEST,
            preferred_element_type=F32,
        )
        / entries
    )
    mean = totals[0:n]
    var = totals[n : 2 * n] - mean * mean
    return mean, lax.rsqrt(var + EPSILON)


def wide_moments(total, square):
    pieces = [total[:, 128 * k : 128 * k + 128] for k in range(4)]
    pieces += [square[:, 128 * k : 128 * k + 128] for k in range(4)]
    mean, rstd = moments(jnp.concatenate(pieces, axis=0), 128, CELLS * WIDTH, 4)
    spread = lambda v: jnp.concatenate([v[k : k + 1] for k in range(4)], axis=1)
    return spread(mean), spread(rstd)


def silu(v):
    return v * (0.5 * jnp.tanh(0.5 * v) + 0.5)


def dot(a, b):
    return jnp.dot(a, b, preferred_element_type=F32)


def dot_t(a, b):
    return lax.dot_general(a, b, (((1,), (1,)), ((), ())), preferred_element_type=F32)


def kernel(
    tok, gain0, wq, wk, wv, wo, gain1, k1, gain2, k2, out,
    xg, x32, nb, wts, wm, wn, w1r, w1t, w2, gains, gain2v, act, zs, sums, hid, msg, acc,
    xown, xrest, ua, in1, in2, rss, rsr, zsend, zrecv, zdirect, near,
    load_sem, ag_send, ag_recv, fx_send, fx_recv, rs_send, rs_recv, z_send, z_recv, zd_send, zd_recv,
):
    me = lax.axis_index("tok")
    f = lax.axis_index("tm")
    frames = lax.axis_size("tm")
    y = me // 2
    h = me % 2
    o = 1 - h
    across = 2 * y + o
    y2 = (y + 2) % 4
    beyond = 2 * y2 + o
    core = f % 2
    mate = f + 1 - 2 * core

    def beside(d):
        return 2 * ((y + d) % 4) + h

    dma = pltpu.make_async_copy

    own = [
        dma(tok.at[0, :, pl.ds(PIECE * k, PIECE)], xg.at[me, k], load_sem.at[11 + k])
        for k in range(PIECES)
    ]
    small = [
        dma(gain0, gains.at[0], load_sem.at[2]),
        dma(gain1, gains.at[1], load_sem.at[3]),
        dma(gain2, gain2v, load_sem.at[4]),
    ]
    mats = [dma(w, wts.at[k], load_sem.at[5 + k]) for k, w in enumerate((wq, wk, wv, wo))]
    barrier = pltpu.get_barrier_semaphore()

    def greet(**there):
        pl.semaphore_signal(barrier, inc=1, device_id=there, device_id_type=MESH)

    def load():
        for c in own:
            c.start()

        greet(tok=across)
        for d in (2, 1, 3):
            greet(tok=beside(d))

        greet(tm=mate)

        @pl.when(f >= 2)
        def _():
            greet(tm=f - 2)

        for c in mats + small:
            c.start()
        for k, (a, b, e) in enumerate(FIRST_ORDER):
            dma(k1.at[a, b, e], w1r.at[pl.ds(LOCAL * k, LOCAL)], load_sem.at[9]).start()
        for k, (a, b, e) in enumerate(SECOND_ORDER):
            dma(k2.at[a, b, e], w2.at[pl.ds(LOCAL * k, LOCAL)], load_sem.at[10]).start()

    def all_entered():
        for c in own:
            c.wait()
        pl.semaphore_wait(barrier, 5 + jnp.where(f < frames - 2, 1, 0))

    def ag(block, half, k, there):
        return pltpu.make_async_remote_copy(
            src_ref=xg.at[block, half],
            dst_ref=xg.at[block, half],
            send_sem=ag_send.at[k],
            recv_sem=ag_recv.at[block, half],
            device_id={"tok": there},
            device_id_type=MESH,
        )

    def ag_wait(block, half):
        ag(block, half, 0, across).wait_recv()

    gathered = []

    def ag_go(block, half, there):
        c = ag(block, half, len(gathered), there)
        c.start()
        gathered.append(c)

    def gather_own():
        for half in range(PIECES):
            ag_go(me, half, across)
            for d in (2, 1, 3):
                ag_go(me, half, beside(d))
            if half + 1 < PIECES:
                gathered[4 * half].wait_send()

    def gather_far():
        for half in range(PIECES):
            ag_wait(across, half)
            for d in (2, 1, 3):
                ag_go(across, half, beside(d))

    def fold_scores():
        for c in mats[:2]:
            c.wait()
        wm[...] = (dot_t(wts[0], wts[1]) * (math.log2(math.e) / math.sqrt(C))).astype(BF16)

    def fold_values():
        for c in mats[2:]:
            c.wait()
        wn[...] = dot(wts[2], wts[3]).astype(BF16)

    def turn_first():
        dma(w1r, w1r, load_sem.at[9]).wait()
        w1t[...] = w1r[...].T

    def gather_rest():
        for side in (h, o):
            for d in (1, 3, 2):
                for half in range(PIECES):
                    ag_wait(2 * ((y + d) % 4) + side, half)

    zero = jnp.zeros((1, C), F32)

    def norm_tokens():
        for c in small:
            c.wait()

        def collect(j, carry):
            total, square = carry
            rows = pl.ds(pl.multiple_of(j * COLS, 8), COLS)
            v = jnp.concatenate([xg[j, k].astype(F32) for k in range(PIECES)], axis=1)
            x32[rows, :] = v
            return (
                total + jnp.sum(v, axis=0, keepdims=True),
                square + jnp.sum(v * v, axis=0, keepdims=True),
            )

        mean, rstd = wide_moments(*lax.fori_loop(0, ROWS, collect, (zero, zero)))
        scale = rstd * gains[0]

        def norm(k, carry):
            rows = pl.ds(pl.multiple_of(k * 208, 16), 208)
            nb[rows, :] = ((x32[rows, :] - mean) * scale).astype(BF16)
            return carry

        lax.fori_loop(0, 4, norm, 0)

    def attention():
        q = dot(nb[...], wm[...]).astype(BF16)
        s = dot_t(q, nb[...])
        p = jnp.exp2(s - jnp.max(s, axis=1, keepdims=True))
        bottom = jnp.sum(p, axis=1, keepdims=True)
        context = (dot(p.astype(BF16), nb[...]) / bottom).astype(BF16)
        v = (x32[...] + dot(context, wn[...])).astype(BF16).astype(F32)
        x32[...] = v
        sums[0] = jnp.sum(v, axis=0, keepdims=True)
        sums[1] = jnp.sum(v * v, axis=0, keepdims=True)

    def activate():
        mean, rstd = wide_moments(sums[0], sums[1])
        scale = rstd * gains[1]

        def one(k, carry):
            rows = pl.ds(pl.multiple_of(k * 208, 16), 208)
            act[rows, :] = silu((x32[rows, :] - mean) * scale).astype(BF16)
            return carry

        lax.fori_loop(0, 4, one, 0)

    def fx(src, dst, there, k, slot):
        return pltpu.make_async_remote_copy(
            src_ref=src,
            dst_ref=dst,
            send_sem=fx_send.at[k],
            recv_sem=fx_recv.at[slot],
            device_id={"tm": there},
            device_id_type=MESH,
        )

    def columns(first, last):
        cols = slice(256 * first, min(256 * last, 27 * LOCAL))
        zs[:, cols] = dot(act[...], w1t[:, cols])

    def fold(time):
        first, last, half = FIRST_PLACES[time]
        z = lambda c, n=128: zs[:, c : c + n].reshape(ROWS, COLS, n)
        low = lane_low((ROWS, COLS, 128))
        shifted = col_before_after(
            row_before(z(first)) + z(first + 128) + row_after(z(first + 256))
        )
        middle = z(first + 384)
        middle = jnp.where(low, row_before(middle), middle)
        if time < 2:
            extra = row_after(z(last))
        else:
            extra = jnp.concatenate(
                [row_after(z(last, 64)), jnp.zeros((ROWS, COLS, 64), F32)], axis=2
            )
        extra = jnp.where(low if half == 0 else ~low, extra, 0.0)
        total = shifted + middle + extra
        total = total + pltpu.roll(total, 64, 2)
        packed = jnp.where(low[0:4], total[0:4], total[4:8])
        return packed.reshape(CELLS // 2, 128)

    def first_one_ahead():
        columns(3, 5)
        msg[0] = fold(1).astype(BF16)

    def one_ahead():
        return fx(msg.at[0], in1.at[0], mate, 0, 0)

    def first_two_ahead():
        columns(0, 3)
        msg[1] = fold(0).astype(BF16)

    def two_ahead():
        return fx(msg.at[1], in1.at[1], f + 2, 1, 1)

    def first_frame():
        return fx(msg.at[2], in1.at[1], mate, 2, 1)

    def send_two_ahead():
        @pl.when(f == 0)
        def _():
            msg[2] = msg[1]
            first_frame().start()

        @pl.when(core == 0)
        def _():
            one_ahead().wait_recv()
            msg[1] = (msg[1].astype(F32) + in1[0].astype(F32)).astype(BF16)

        @pl.when(f < frames - 2)
        def _():
            two_ahead().start()

    def send_one_ahead():
        one_ahead().start()

        @pl.when(f == 0)
        def _():
            in1[1] = (msg[0].astype(F32) + msg[2].astype(F32)).astype(BF16)

    def first_own():
        columns(5, 7)
        hid[...] = fold(2)

    def wait_first():
        @pl.when(core == 1)
        def _():
            one_ahead().wait_recv()

        @pl.when(f >= 1)
        def _():
            two_ahead().wait_recv()

    def activate_second():
        hidden = hid[...] + in1[1].astype(F32) + jnp.where(core == 1, in1[0].astype(F32), 0.0)
        pieces = [
            jnp.sum(hidden, axis=0, keepdims=True),
            jnp.sum(hidden * hidden, axis=0, keepdims=True),
            jnp.zeros((6, 128), F32),
        ]
        mean, rstd = moments(jnp.concatenate(pieces, axis=0), 64, CELLS * WIDTH, 1)
        gain = jnp.concatenate([gain2v[...], gain2v[...]], axis=1)
        ua[...] = silu((hidden - mean) * (rstd * gain)).astype(BF16)

    def near_second():
        return fx(ua, in2.at[0], mate, 3, 2)

    def far_second():
        return fx(ua, in2.at[1], f + 2, 4, 3)

    def passed_second():
        return fx(in2.at[1], in2.at[0], mate, 3, 2)

    def send_second():
        @pl.when(f < frames - 2)
        def _():
            far_second().start()

        @pl.when(core == 0)
        def _():
            near_second().start()

        @pl.when(f == 0)
        def _():
            in2[0] = ua[...]
            in2[1] = ua[...]

    def spread(dense):
        d = dense.astype(F32).reshape(4, COLS, 128)
        low = lane_low((4, COLS, 128))
        other = pltpu.roll(d, 64, 2)
        both = jnp.concatenate([jnp.where(low, d, other), jnp.where(low, other, d)], axis=0)
        sides = col_before_after(both)
        flat = lambda v: jnp.concatenate([v[r : r + 1] for r in ORDER], axis=0).reshape(CELLS, 128)
        wide = [
            flat(row_before(sides)),
            flat(sides),
            flat(row_after(sides)),
            flat(jnp.where(lane_low(both.shape), row_before(both), both)),
        ]
        return wide, flat(row_after(both))

    def second_own():
        dma(w2, w2, load_sem.at[10]).wait()
        wide, last = spread(ua[...])
        for k in range(4):
            xown[:, 128 * k : 128 * k + 128] = wide[k].astype(BF16)
        xrest[:, 1152:1216] = last[:, 0:64].astype(BF16)

        acc[...] = dot(xown[...], w2[0:512, :])

    passes = jnp.logical_and(core == 1, f >= 3)

    def wait_second():
        @pl.when(f >= 2)
        def _():
            far_second().wait_recv()

        @pl.when(passes)
        def _():
            passed_second().start()

        @pl.when(f == 1)
        def _():
            near_second().wait_recv()
            in2[1] = in2[0]

    def second_back():
        wide, last0 = spread(in2[1])
        for k in range(4):
            xrest[:, 128 * k : 128 * k + 128] = wide[k].astype(BF16)
        acc[...] = acc[...] + dot(xrest[:, 0:512], w2[512:1024, :])

        @pl.when(f >= 2)
        def _():
            near_second().wait_recv()

        wide, last1 = spread(in2[0])
        for k in range(4):
            xrest[:, 512 + 128 * k : 640 + 128 * k] = wide[k].astype(BF16)
        xrest[:, 1024:1152] = jnp.where(lane_low(last0.shape), last1, last0).astype(BF16)

    half_frame = CELLS // 2
    scattered = []

    def rs(r, half, d):
        return pltpu.make_async_remote_copy(
            src_ref=rss.at[r, half, (y + d) % 4],
            dst_ref=rsr.at[r, half, d - 1],
            send_sem=rs_send.at[r, half, d - 1],
            recv_sem=rs_recv.at[r, half, d - 1],
            device_id={"tok": beside(d)},
            device_id_type=MESH,
        )

    def sum_rows(r, side, half):
        rows = pl.ds(pl.multiple_of(side * half_frame, 16), half_frame)
        cols = slice(PART * half, PART * half + PART)
        v = acc[rows, cols] + dot(xrest[rows, 512:1216], w2[1024:1728, cols])
        acc[rows, cols] = v
        rss[r, half] = v.reshape(4, COLS, PART).astype(BF16)

    def direct(half):
        return pltpu.make_async_remote_copy(
            src_ref=rss.at[0, half, y2],
            dst_ref=zdirect.at[half],
            send_sem=zd_send.at[half],
            recv_sem=zd_recv.at[half],
            device_id={"tok": beyond},
            device_id_type=MESH,
        )

    def send_rows(r, half):
        for d in (1, 3) if r == 0 else (2, 1, 3):
            c = rs(r, half, d)
            c.start()
            scattered.append(c)
        if r == 0:
            direct(half).start()

    def home(half):
        return pltpu.make_async_remote_copy(
            src_ref=zsend.at[half],
            dst_ref=zrecv.at[half],
            send_sem=z_send.at[half],
            recv_sem=z_recv.at[half],
            device_id={"tok": across},
            device_id_type=MESH,
        )

    def collect_rows(r, side, half):
        come = (1, 3) if r == 0 else (1, 3, 2)
        for d in come:
            rs(r, half, d).wait_recv()
        rows = pl.ds(pl.multiple_of(side * half_frame + y * COLS, 8), COLS)
        cols = slice(PART * half, PART * half + PART)
        v = acc[rows, cols]
        for d in come:
            v = v + rsr[r, half, d - 1].astype(F32)
        return v

    def scatter():
        for half in range(PARTS):
            sum_rows(0, o, half)
            send_rows(0, half)
        for half in range(PARTS):
            sum_rows(1, h, half)
        for half in range(PARTS):
            send_rows(1, half)
        for half in range(PARTS):
            zsend[half] = collect_rows(0, o, half).astype(BF16)
            home(half).start()
        own_rows = pl.ds(pl.multiple_of(me * COLS, 8), COLS)
        for half in range(PARTS):
            cols = slice(PART * half, PART * half + PART)
            near[half] = collect_rows(1, h, half) + x32[own_rows, cols]

    def last():
        for half in range(PARTS):
            cols = slice(PART * half, PART * half + PART)
            direct(half).wait_recv()
            v = near[half] + zdirect[half].astype(F32)
            home(half).wait_recv()
            out[0, :, cols] = (v + zrecv[half].astype(F32)).astype(BF16)

    def finish():
        for k, c in enumerate(gathered + scattered):
            if k >= 4 * PIECES or k % 4 or k == 4 * (PIECES - 1):
                c.wait_send()

    def finish_home():
        for half in range(PARTS):
            home(half).wait_send()
            direct(half).wait_send()

    def finish_frames():
        one_ahead().wait_send()

        @pl.when(f < frames - 2)
        def _():
            two_ahead().wait_send()
            far_second().wait_send()

        @pl.when(f == 0)
        def _():
            first_frame().wait_send()

        @pl.when(core == 0)
        def _():
            near_second().wait_send()

        @pl.when(passes)
        def _():
            passed_second().wait_send()

    load()
    all_entered()
    gather_own()
    fold_scores()
    fold_values()
    gather_far()
    turn_first()
    gather_rest()
    norm_tokens()
    attention()
    activate()
    first_two_ahead()
    send_two_ahead()
    first_one_ahead()
    send_one_ahead()
    first_own()
    wait_first()
    activate_second()
    send_second()
    second_own()
    wait_second()
    second_back()
    scatter()
    last()
    finish()
    finish_home()
    finish_frames()


def per_device(tokens, gain0, wq, wk, wv, wo, gain1, k1, gain2, k2):
    dma = pltpu.SemaphoreType.DMA
    vmem = pltpu.VMEM
    return pl.pallas_call(
        kernel,
        out_shape=pltpu.VMEM((1, COLS, C), BF16),
        in_specs=[pl.BlockSpec(memory_space=pl.ANY)] * 10,
        out_specs=pl.BlockSpec(memory_space=pltpu.VMEM),
        scratch_shapes=[
            vmem((ROWS, PIECES, COLS, PIECE), BF16),
            vmem((CELLS, C), F32),
            vmem((CELLS, C), BF16),
            vmem((4, C, C), BF16),
            vmem((C, C), BF16),
            vmem((C, C), BF16),
            vmem((27 * LOCAL, C), BF16),
            vmem((C, 27 * LOCAL), BF16),
            vmem((27 * LOCAL, C), BF16),
            vmem((2, 1, C), F32),
            vmem((1, LOCAL), F32),
            vmem((CELLS, C), BF16),
            vmem((CELLS, 27 * LOCAL), F32),
            vmem((2, 1, C), F32),
            vmem((CELLS // 2, 128), F32),
            vmem((3, CELLS // 2, 128), BF16),
            vmem((CELLS, C), F32),
            vmem((CELLS, C), BF16),
            vmem((CELLS, 19 * LOCAL), BF16),
            vmem((CELLS // 2, 128), BF16),
            vmem((2, CELLS // 2, 128), BF16),
            vmem((2, CELLS // 2, 128), BF16),
            vmem((2, PARTS, 4, COLS, PART), BF16),
            vmem((2, PARTS, 3, COLS, PART), BF16),
            vmem((PARTS, COLS, PART), BF16),
            vmem((PARTS, COLS, PART), BF16),
            vmem((PARTS, COLS, PART), BF16),
            vmem((PARTS, COLS, PART), F32),
            dma((11 + PIECES,)),
            dma((7 * PIECES,)),
            dma((ROWS, PIECES)),
            dma((5,)),
            dma((4,)),
            dma((2, PARTS, 3)),
            dma((2, PARTS, 3)),
            dma((PARTS,)),
            dma((PARTS,)),
            dma((PARTS,)),
            dma((PARTS,)),
        ],
        compiler_params=pltpu.CompilerParams(
            collective_id=0, has_side_effects=True, vmem_limit_bytes=56 * 2**20
        ),
    )(
        tokens,
        gain0.reshape(1, C),
        wq,
        wk,
        wv,
        wo,
        gain1.reshape(1, C),
        jnp.swapaxes(k1, 3, 4),
        gain2.reshape(1, LOCAL),
        k2,
    )


def solution(mesh):
    placed = (
        P("tm", "tok", None),
        P(),
        P(),
        P(),
        P(),
        P(),
        P(),
        P(None, None, None, None, "tok"),
        P("tok"),
        P(None, None, None, "tok", None),
    )
    return jax.shard_map(
        per_device, mesh=mesh, in_specs=placed, out_specs=P("tm", "tok", None), check_vma=False
    )
```

```python
import math

import jax
import jax.numpy as jnp
from jax import lax
from jax.experimental import pallas as pl
from jax.experimental.pallas import tpu as pltpu
from jax.sharding import PartitionSpec as P

F32 = jnp.float32
BF16 = jnp.bfloat16
MESH = pl.DeviceIdType.MESH

C = 512
PIECES = 2
PIECE = C // PIECES
PARTS = 2
PART = C // PARTS
ROWS = 8
COLS = 104
CELLS = ROWS * COLS
WIDTH = 16
LOCAL = 64
EPSILON = 1e-06

ORDER = (0, 2, 4, 6, 1, 3, 5, 7)

PAIRS = ((0, 0), (0, 2), (1, 0), (1, 2), (2, 0), (2, 2), (0, 1), (1, 1))
LAST = (2, 1)


def taps_of(time):
    return tuple((time,) + pair for pair in PAIRS)


FIRST_ORDER = (
    taps_of(0) + ((0,) + LAST, (1,) + LAST) + taps_of(1) + taps_of(2) + ((2,) + LAST,)
)
SECOND_ORDER = (
    taps_of(2) + taps_of(0) + taps_of(1) + ((1,) + LAST, (0,) + LAST, (2,) + LAST)
)
FIRST_PLACES = ((0, 512, 0), (640, 512, 1), (1152, 1664, 0))


def lane_low(shape):
    return lax.broadcasted_iota(jnp.int32, shape, len(shape) - 1) < 64


def row_before(x):
    return jnp.concatenate([x[0:1], x[0 : ROWS - 1]], axis=0)


def row_after(x):
    return jnp.concatenate([x[1:ROWS], x[ROWS - 1 : ROWS]], axis=0)


def col_before_after(x):
    col = lax.broadcasted_iota(jnp.int32, x.shape, 1)
    before = jnp.where(col == 0, x, pltpu.roll(x, 1, 1))
    after = jnp.where(col == COLS - 1, x, pltpu.roll(x, COLS - 1, 1))
    return jnp.where(lane_low(x.shape), before, after)


def group_matrix(period):
    i = lax.broadcasted_iota(jnp.int32, (128, 128), 0)
    k = lax.broadcasted_iota(jnp.int32, (128, 128), 1)
    same = ((i & (period - 1)) >> 4) == ((k & (period - 1)) >> 4)
    return jnp.where(same, 1.0, 0.0).astype(BF16)


def moments(stacked, period, entries, n):
    high = stacked.astype(BF16).astype(F32)
    rest = stacked - high
    middle = rest.astype(BF16).astype(F32)
    terms = jnp.concatenate([high, middle, rest - middle], axis=0).astype(BF16)
    grouped = dot(terms, group_matrix(period))
    totals = (grouped[0:8] + grouped[8:16] + grouped[16:24]) / entries
    mean = totals[0:n]
    var = totals[n : 2 * n] - mean * mean
    return mean, lax.rsqrt(var + EPSILON)


def wide_moments(total, square):
    pieces = [total[:, 128 * k : 128 * k + 128] for k in range(4)]
    pieces += [square[:, 128 * k : 128 * k + 128] for k in range(4)]
    mean, rstd = moments(jnp.concatenate(pieces, axis=0), 128, CELLS * WIDTH, 4)
    spread = lambda v: jnp.concatenate([v[k : k + 1] for k in range(4)], axis=1)
    return spread(mean), spread(rstd)


def silu_of_twice(w):
    return w * jnp.tanh(w) + w


def dot(a, b):
    return jnp.dot(a, b, preferred_element_type=F32)


def dot_t(a, b):
    return lax.dot_general(a, b, (((1,), (1,)), ((), ())), preferred_element_type=F32)


def kernel(
    tok, gain0, wq, wk, wv, wo, gain1, k1, gain2, k2, out,
    xg, x32, nb, wts, wm, wn, w1r, w1t, w2, gains, gain2v, act, zs, sums, part, hid, msg, acc,
    xown, xrest, ua, in1, in2, rss, rsr, zsend, zrecv, near,
    in_sem, load_sem, ag_send, ag_recv, fx_send, fx_recv, rs_send, rs_recv, z_send, z_recv,
):
    me = lax.axis_index("tok")
    f = lax.axis_index("tm")
    frames = lax.axis_size("tm")
    y = me // 2
    h = me % 2
    o = 1 - h
    across = 2 * y + o
    core = f % 2
    mate = f + 1 - 2 * core
    leaves = jnp.logical_and(f % 8 >= 6, f < frames - 2)
    enters = jnp.logical_and(f % 8 < 2, f >= 8)

    def beside(d):
        return 2 * ((y + d) % 4) + h

    dma = pltpu.make_async_copy

    own = [
        dma(tok.at[0, :, pl.ds(PIECE * k, PIECE)], xg.at[me, k], load_sem.at[11 + k])
        for k in range(PIECES)
    ]
    small = [
        dma(gain0, gains.at[0], load_sem.at[2]),
        dma(gain1, gains.at[1], load_sem.at[3]),
        dma(gain2, gain2v, load_sem.at[4]),
    ]
    mats = [dma(w, wts.at[k], load_sem.at[5 + k]) for k, w in enumerate((wq, wk, wv, wo))]
    barrier = pltpu.get_barrier_semaphore()

    def greet(**there):
        pl.semaphore_signal(barrier, inc=1, device_id=there, device_id_type=MESH)

    def load():
        for c in own:
            c.start()

        greet(tok=across)
        for d in (2, 1, 3):
            greet(tok=beside(d))

        greet(tm=mate)

        @pl.when(f >= 2)
        def _():
            greet(tm=f - 2, tok=jnp.where(enters, across, me))

        @pl.when(leaves)
        def _():
            greet(tm=f + 2, tok=across)

        for c in mats + small:
            c.start()
        for k, (a, b, e) in enumerate(FIRST_ORDER):
            dma(k1.at[a, b, e], w1r.at[pl.ds(LOCAL * k, LOCAL)], load_sem.at[9]).start()
        for k, (a, b, e) in enumerate(SECOND_ORDER):
            dma(k2.at[a, b, e], w2.at[pl.ds(LOCAL * k, LOCAL)], load_sem.at[10]).start()

    def all_entered():
        for c in own:
            c.wait()
        nexts = jnp.where(f < frames - 2, 1, 0) + jnp.where(enters, 1, 0)
        pl.semaphore_wait(barrier, 5 + nexts)

        @pl.when(enters)
        def _():
            pl.semaphore_signal(
                in_sem, inc=1, device_id={"tm": f - 2, "tok": across}, device_id_type=MESH
            )


    def ag(block, half, k, there):
        return pltpu.make_async_remote_copy(
            src_ref=xg.at[block, half],
            dst_ref=xg.at[block, half],
            send_sem=ag_send.at[k],
            recv_sem=ag_recv.at[block, half],
            device_id={"tok": there},
            device_id_type=MESH,
        )

    def ag_wait(block, half):
        ag(block, half, 0, across).wait_recv()

    gathered = []

    def ag_go(block, half, there):
        c = ag(block, half, len(gathered), there)
        c.start()
        gathered.append(c)

    def gather_own():
        for half in range(PIECES):
            ag_go(me, half, across)
            for d in (2, 1, 3):
                ag_go(me, half, beside(d))
            if half + 1 < PIECES:
                gathered[4 * half].wait_send()

    def gather_far():
        for half in range(PIECES):
            ag_wait(across, half)
            for d in (2, 1, 3):
                ag_go(across, half, beside(d))

    def fold_scores():
        for c in mats[:2]:
            c.wait()
        wm[...] = (dot_t(wts[0], wts[1]) * (math.log2(math.e) / math.sqrt(C))).astype(BF16)

    def fold_values():
        for c in mats[2:]:
            c.wait()
        wn[...] = dot(wts[2], wts[3]).astype(BF16)

    def turn_first():
        dma(w1r, w1r, load_sem.at[9]).wait()
        w1t[...] = w1r[...].T

    def collect(block):
        v = jnp.concatenate([xg[block, k].astype(F32) for k in range(PIECES)], axis=1)
        x32[pl.ds(pl.multiple_of(block * COLS, 8), COLS), :] = v
        v = v.reshape(COLS // 8, 8, C)
        part[0] = part[0] + jnp.sum(v, axis=0)
        part[1] = part[1] + jnp.sum(v * v, axis=0)

    def collect_here():
        part[...] = jnp.zeros((2, 8, C), F32)
        collect(me)

    def collect_side(side):
        def one(d, carry):
            block = 2 * ((y + d) % 4) + side
            for half in range(PIECES):
                ag_wait(block, half)
            collect(block)
            return carry

        lax.fori_loop(1, 4, one, 0)

    def norm_tokens():
        for c in small:
            c.wait()

        total, square = (jnp.sum(part[k], axis=0, keepdims=True) for k in range(2))
        mean, rstd = wide_moments(total, square)
        scale = rstd * gains[0]

        def norm(k, carry):
            rows = pl.ds(pl.multiple_of(k * 208, 16), 208)
            nb[rows, :] = ((x32[rows, :] - mean) * scale).astype(BF16)
            return carry

        lax.fori_loop(0, 4, norm, 0)

    def attention():
        q = dot(nb[...], wm[...]).astype(BF16)
        s = dot_t(q, nb[...])
        p = jnp.exp2(s - jnp.max(s, axis=1, keepdims=True))
        bottom = jnp.sum(p, axis=1, keepdims=True)
        context = (dot(p.astype(BF16), nb[...]) / bottom).astype(BF16)
        v = (x32[...] + dot(context, wn[...])).astype(BF16).astype(F32)
        x32[...] = v
        sums[0] = jnp.sum(v, axis=0, keepdims=True)
        sums[1] = jnp.sum(v * v, axis=0, keepdims=True)

    def activate():
        mean, rstd = wide_moments(sums[0], sums[1])
        scale = rstd * gains[1] * 0.5

        def one(k, carry):
            rows = pl.ds(pl.multiple_of(k * 208, 16), 208)
            act[rows, :] = silu_of_twice((x32[rows, :] - mean) * scale).astype(BF16)
            return carry

        lax.fori_loop(0, 4, one, 0)

    def fx(src, dst, there, k, slot):
        return pltpu.make_async_remote_copy(
            src_ref=src,
            dst_ref=dst,
            send_sem=fx_send.at[k],
            recv_sem=fx_recv.at[slot],
            device_id={"tm": there},
            device_id_type=MESH,
        )

    def columns(first, last):
        cols = slice(256 * first, min(256 * last, 27 * LOCAL))
        zs[:, cols] = dot(act[...], w1t[:, cols])

    def fold(time):
        first, last, half = FIRST_PLACES[time]
        z = lambda c, n=128: zs[:, c : c + n].reshape(ROWS, COLS, n)
        low = lane_low((ROWS, COLS, 128))
        shifted = col_before_after(
            row_before(z(first)) + z(first + 128) + row_after(z(first + 256))
        )
        middle = z(first + 384)
        middle = jnp.where(low, row_before(middle), middle)
        if time < 2:
            extra = row_after(z(last))
        else:
            extra = jnp.concatenate(
                [row_after(z(last, 64)), jnp.zeros((ROWS, COLS, 64), F32)], axis=2
            )
        extra = jnp.where(low if half == 0 else ~low, extra, 0.0)
        total = shifted + middle + extra
        total = total + pltpu.roll(total, 64, 2)
        packed = jnp.where(low[0:4], total[0:4], total[4:8])
        return packed.reshape(CELLS // 2, 128)

    def first_one_ahead():
        columns(3, 5)
        msg[0] = fold(1).astype(BF16)

    def one_ahead():
        return fx(msg.at[0], in1.at[0], mate, 0, 0)

    def first_two_ahead():
        columns(0, 3)
        msg[1] = fold(0).astype(BF16)

    def two_ahead():
        return fx(msg.at[1], in1.at[1], f + 2, 1, 1)

    def first_frame():
        return fx(msg.at[2], in1.at[1], mate, 2, 1)

    def send_two_ahead():
        @pl.when(f == 0)
        def _():
            msg[2] = msg[1]
            first_frame().start()

        @pl.when(core == 0)
        def _():
            one_ahead().wait_recv()
            msg[1] = (msg[1].astype(F32) + in1[0].astype(F32)).astype(BF16)

        @pl.when(leaves)
        def _():
            pl.semaphore_wait(in_sem, 1)

        @pl.when(f < frames - 2)
        def _():
            two_ahead().start()

    def send_one_ahead():
        one_ahead().start()

        @pl.when(f == 0)
        def _():
            in1[1] = (msg[0].astype(F32) + msg[2].astype(F32)).astype(BF16)

    def first_own():
        columns(5, 7)
        hid[...] = fold(2)

    def wait_first():
        @pl.when(core == 1)
        def _():
            one_ahead().wait_recv()

        @pl.when(f >= 1)
        def _():
            two_ahead().wait_recv()

    def activate_second():
        hidden = hid[...] + in1[1].astype(F32) + jnp.where(core == 1, in1[0].astype(F32), 0.0)
        pieces = [
            jnp.sum(hidden, axis=0, keepdims=True),
            jnp.sum(hidden * hidden, axis=0, keepdims=True),
            jnp.zeros((6, 128), F32),
        ]
        mean, rstd = moments(jnp.concatenate(pieces, axis=0), 64, CELLS * WIDTH, 1)
        gain = jnp.concatenate([gain2v[...], gain2v[...]], axis=1)
        ua[...] = silu_of_twice((hidden - mean) * (rstd * gain * 0.5)).astype(BF16)

    def near_second():
        return fx(ua, in2.at[0], mate, 3, 2)

    def far_second():
        return fx(ua, in2.at[1], f + 2, 4, 3)

    def passed_second():
        return fx(in2.at[1], in2.at[0], mate, 3, 2)

    def send_second():
        @pl.when(f < frames - 2)
        def _():
            far_second().start()

        @pl.when(core == 0)
        def _():
            near_second().start()

        @pl.when(f == 0)
        def _():
            in2[0] = ua[...]
            in2[1] = ua[...]

    def spread(dense):
        d = dense.astype(F32).reshape(4, COLS, 128)
        low = lane_low((4, COLS, 128))
        other = pltpu.roll(d, 64, 2)
        both = jnp.concatenate([jnp.where(low, d, other), jnp.where(low, other, d)], axis=0)
        sides = col_before_after(both)
        flat = lambda v: jnp.concatenate([v[r : r + 1] for r in ORDER], axis=0).reshape(CELLS, 128)
        wide = [
            flat(row_before(sides)),
            flat(sides),
            flat(row_after(sides)),
            flat(jnp.where(lane_low(both.shape), row_before(both), both)),
        ]
        return wide, flat(row_after(both))

    def second_own():
        dma(w2, w2, load_sem.at[10]).wait()
        wide, last = spread(ua[...])
        for k in range(4):
            xown[:, 128 * k : 128 * k + 128] = wide[k].astype(BF16)
        xrest[:, 1152:1216] = last[:, 0:64].astype(BF16)

        acc[...] = dot(xown[...], w2[0:512, :])

    passes = jnp.logical_and(core == 1, f >= 3)

    def wait_second():
        @pl.when(f >= 2)
        def _():
            far_second().wait_recv()

        @pl.when(passes)
        def _():
            passed_second().start()

        @pl.when(f == 1)
        def _():
            near_second().wait_recv()
            in2[1] = in2[0]

    def second_back():
        wide, last0 = spread(in2[1])
        for k in range(4):
            xrest[:, 128 * k : 128 * k + 128] = wide[k].astype(BF16)
        acc[...] = acc[...] + dot(xrest[:, 0:512], w2[512:1024, :])

        @pl.when(f >= 2)
        def _():
            near_second().wait_recv()

        wide, last1 = spread(in2[0])
        for k in range(4):
            xrest[:, 512 + 128 * k : 640 + 128 * k] = wide[k].astype(BF16)
        xrest[:, 1024:1152] = jnp.where(lane_low(last0.shape), last1, last0).astype(BF16)

    half_frame = CELLS // 2
    scattered = []

    def rs(r, half, d):
        return pltpu.make_async_remote_copy(
            src_ref=rss.at[r, half, (y + d) % 4],
            dst_ref=rsr.at[r, half, d - 1],
            send_sem=rs_send.at[r, half, d - 1],
            recv_sem=rs_recv.at[r, half, d - 1],
            device_id={"tok": beside(d)},
            device_id_type=MESH,
        )

    def sum_rows(r, side, half):
        rows = pl.ds(pl.multiple_of(side * half_frame, 16), half_frame)
        cols = slice(PART * half, PART * half + PART)
        v = acc[rows, cols] + dot(xrest[rows, 512:1216], w2[1024:1728, cols])
        acc[rows, cols] = v
        rss[r, half] = v.reshape(4, COLS, PART).astype(BF16)

    def send_rows(r, half):
        for d in (2, 1, 3):
            c = rs(r, half, d)
            c.start()
            scattered.append(c)

    def home(half):
        return pltpu.make_async_remote_copy(
            src_ref=zsend.at[half],
            dst_ref=zrecv.at[half],
            send_sem=z_send.at[half],
            recv_sem=z_recv.at[half],
            device_id={"tok": across},
            device_id_type=MESH,
        )

    def collect_rows(r, side, half):
        for d in (1, 3, 2):
            rs(r, half, d).wait_recv()
        rows = pl.ds(pl.multiple_of(side * half_frame + y * COLS, 8), COLS)
        cols = slice(PART * half, PART * half + PART)
        v = acc[rows, cols]
        for d in (1, 2, 3):
            v = v + rsr[r, half, d - 1].astype(F32)
        return v

    def scatter():
        for half in range(PARTS):
            sum_rows(0, o, half)
            send_rows(0, half)
        for half in range(PARTS):
            sum_rows(1, h, half)
        for half in range(PARTS):
            send_rows(1, half)
        for half in range(PARTS):
            zsend[half] = collect_rows(0, o, half).astype(BF16)
            home(half).start()
        own_rows = pl.ds(pl.multiple_of(me * COLS, 8), COLS)
        for half in range(PARTS):
            cols = slice(PART * half, PART * half + PART)
            near[half] = collect_rows(1, h, half) + x32[own_rows, cols]

    def last():
        for half in range(PARTS):
            cols = slice(PART * half, PART * half + PART)
            home(half).wait_recv()
            out[0, :, cols] = (near[half] + zrecv[half].astype(F32)).astype(BF16)

    def finish():
        for k, c in enumerate(gathered + scattered):
            if k >= 4 * PIECES or k % 4 or k == 4 * (PIECES - 1):
                c.wait_send()

    def finish_home():
        for half in range(PARTS):
            home(half).wait_send()

    def finish_frames():
        one_ahead().wait_send()

        @pl.when(f < frames - 2)
        def _():
            two_ahead().wait_send()
            far_second().wait_send()

        @pl.when(f == 0)
        def _():
            first_frame().wait_send()

        @pl.when(core == 0)
        def _():
            near_second().wait_send()

        @pl.when(passes)
        def _():
            passed_second().wait_send()

    load()
    all_entered()
    gather_own()
    collect_here()
    fold_scores()
    fold_values()
    gather_far()
    turn_first()
    collect_side(h)
    collect(across)
    collect_side(o)
    norm_tokens()
    attention()
    activate()
    first_two_ahead()
    send_two_ahead()
    first_one_ahead()
    send_one_ahead()
    first_own()
    wait_first()
    activate_second()
    send_second()
    second_own()
    wait_second()
    second_back()
    scatter()
    finish()
    finish_frames()
    last()
    finish_home()


def per_device(tokens, gain0, wq, wk, wv, wo, gain1, k1, gain2, k2):
    dma = pltpu.SemaphoreType.DMA
    vmem = pltpu.VMEM
    return pl.pallas_call(
        kernel,
        out_shape=pltpu.VMEM((1, COLS, C), BF16),
        in_specs=[pl.BlockSpec(memory_space=pl.ANY)] * 10,
        out_specs=pl.BlockSpec(memory_space=pltpu.VMEM),
        scratch_shapes=[
            vmem((ROWS, PIECES, COLS, PIECE), BF16),
            vmem((CELLS, C), F32),
            vmem((CELLS, C), BF16),
            vmem((4, C, C), BF16),
            vmem((C, C), BF16),
            vmem((C, C), BF16),
            vmem((27 * LOCAL, C), BF16),
            vmem((C, 27 * LOCAL), BF16),
            vmem((27 * LOCAL, C), BF16),
            vmem((2, 1, C), F32),
            vmem((1, LOCAL), F32),
            vmem((CELLS, C), BF16),
            vmem((CELLS, 27 * LOCAL), F32),
            vmem((2, 1, C), F32),
            vmem((2, 8, C), F32),
            vmem((CELLS // 2, 128), F32),
            vmem((3, CELLS // 2, 128), BF16),
            vmem((CELLS, C), F32),
            vmem((CELLS, C), BF16),
            vmem((CELLS, 19 * LOCAL), BF16),
            vmem((CELLS // 2, 128), BF16),
            vmem((2, CELLS // 2, 128), BF16),
            vmem((2, CELLS // 2, 128), BF16),
            vmem((2, PARTS, 4, COLS, PART), BF16),
            vmem((2, PARTS, 3, COLS, PART), BF16),
            vmem((PARTS, COLS, PART), BF16),
            vmem((PARTS, COLS, PART), BF16),
            vmem((PARTS, COLS, PART), F32),
            pltpu.SemaphoreType.REGULAR,
            dma((11 + PIECES,)),
            dma((7 * PIECES,)),
            dma((ROWS, PIECES)),
            dma((5,)),
            dma((4,)),
            dma((2, PARTS, 3)),
            dma((2, PARTS, 3)),
            dma((PARTS,)),
            dma((PARTS,)),
        ],
        compiler_params=pltpu.CompilerParams(
            collective_id=0, has_side_effects=True, vmem_limit_bytes=56 * 2**20
        ),
    )(
        tokens,
        gain0.reshape(1, C),
        wq,
        wk,
        wv,
        wo,
        gain1.reshape(1, C),
        jnp.swapaxes(k1, 3, 4),
        gain2.reshape(1, LOCAL),
        k2,
    )


def solution(mesh):
    placed = (
        P("tm", "tok", None),
        P(),
        P(),
        P(),
        P(),
        P(),
        P(),
        P(None, None, None, None, "tok"),
        P("tok"),
        P(None, None, None, "tok", None),
    )
    return jax.shard_map(
        per_device, mesh=mesh, in_specs=placed, out_specs=P("tm", "tok", None), check_vma=False
    )
```
